768 devices in a mesh: dp: 16 (over y_lo, x), expert: 48 (over z, y_hi, core).
Axes of the slice: x: 4, y: 8 (y_hi: 2, y_lo: 4; y = y_hi * 4 + y_lo), z: 12, core: 2. Of those that a mesh axis runs over, the one named last changes fastest.
Arguments:
- tokens: bfloat16 [98304, 1024], P(('dp', 'expert')), may hold values from -6 to 6
- upstream: bfloat16 [98304, 1024], P(('dp', 'expert')), may hold values from -6 to 6
- task_ids: int32 [98304, 1], P(('dp', 'expert')), may hold values from 0 to 47; in each aligned block of 128 rows (0 to 127, 128 to 255, ...) at most 3 rows name the same one
- task_expert: int32 [48], replicated, may hold values from 0 to 47, each once
- w_in: bfloat16 [48, 1024, 4096], P('expert', None, 'dp'), may hold values from -0.1875 to 0.1875
- w_out: bfloat16 [48, 4096, 1024], P('expert', 'dp'), may hold values from -0.09375 to 0.09375
Outputs:
- token_grad: bfloat16 [98304, 1024], P(('dp', 'expert'))
- grad_in: float32 [48, 1024, 4096], P('expert', None, 'dp')
- grad_out: float32 [48, 4096, 1024], P('expert', 'dp')
The draws below stay inside these ranges and needn't reach their ends.
Inputs may be any that keep to these rules, and one draw needn't show every extreme that they name: `task_ids`: among the 128 rows of one device no task appears more than 3 times, and some task appears exactly 3 times in the rows of some device. `task_expert`: each expert is the expert of exactly one task.
All inputs are finite; a program needn't handle non-finite values.
Results may differ from the reference program's by a relative error of at most 0.023.
Values may be sent and summed in bfloat16 or wider, within the bound.
No kernel may reach another device: no remote copies, remote signals or barrier semaphores. Data moves between devices by JAX's collectives and lax.ppermute only.
A program may use at most 64 MiB of HBM per device.

```python
import math
import jax
import jax.numpy as jnp
import numpy as np
from jax import lax

D = 1024
FF = 4096
TOK_DEV = 128
EXPERTS = 48
CAP = 3
FF_DEV = 256
TOKENS = 98304
N_DP = 16
N_EXPERT = 48


def shard_levels(rng, dims, split, least, top_value):
    def one(axis_at, parts):
        steps = jax.random.uniform(jax.random.fold_in(jax.random.fold_in(rng, 6), axis_at), (parts,), jnp.float32, least / len(split), top_value / len(split))
        return jnp.repeat(jnp.exp(steps), dims[axis_at] // parts).reshape((-1,) + (1,) * (len(dims) - axis_at - 1))

    factor_of = one(*split[0])
    for cut in split[1:]:
        factor_of = factor_of * one(*cut)
    return factor_of


def assign_block(key, own, number, rows, number_of, top, limit, lean):
    sequence = jax.random.permutation(key, number_of)
    heavy_load, ordinary = load_shares(number_of, rows * top, limit, lean, True), load_shares(number_of, rows * top, limit, lean, False)
    places = jnp.arange(number_of)

    def named(sizes, offset_by):
        used = int((sizes > 0).sum())
        fixed = max(1, used // 4)
        shifted = fixed + (places - fixed + offset_by * (used - fixed)) % max(1, number_of - fixed)
        return jnp.zeros((number_of,), jnp.int32).at[sequence[jnp.where(places < fixed, places, shifted)]].set(jnp.asarray(sizes, jnp.int32))

    sizes = jnp.where(number % 4 == 0, named(heavy_load, number // 4), named(ordinary, number - number // 4 - 1))
    mixed = jax.random.permutation(jax.random.fold_in(own, 3), number_of)
    giver, sink = mixed[0:number_of // 2 * 2:2], mixed[1:number_of // 2 * 2:2]
    slack = jnp.minimum(sizes[giver] - 1, limit - sizes[sink]) // 2
    slack = jnp.where((giver == sequence[0]) | (sink == sequence[0]) | (sizes[sink] == 0), 0, jnp.maximum(slack, 0))
    shifted = jax.random.randint(jax.random.fold_in(own, 4), (number_of // 2,), 0, 1 << 20) % (slack + 1)
    sizes = sizes.at[giver].add(-shifted).at[sink].add(shifted)
    labels = jnp.searchsorted(jnp.cumsum(sizes), jnp.arange(rows * top), side="right").astype(jnp.int32)
    grid = labels.reshape(top, rows).T
    grid = grid[jax.random.permutation(jax.random.fold_in(own, 1), rows)]
    offset_by = jax.random.randint(jax.random.fold_in(own, 2), (rows, 1), 0, top)
    return jnp.take_along_axis(grid, (jnp.arange(top)[None, :] + offset_by) % top, axis=1)


def load_shares(amount, total, bound, skew, full):
    weights = [(1 << 20) // math.isqrt(grade ** skew) + 1 for grade in range(1, amount + 1)]
    largest = bound if full else min(bound, max(-(-total // amount), total * weights[0] // sum(weights)))
    least = 1 if total - largest >= amount - 1 else 0
    given, surplus = [largest] + [least] * (amount - 1), total - largest - least * (amount - 1)
    while surplus > 0:
        movable = [i for i in range(1, amount) if given[i] < largest] or [i for i in range(1, amount) if given[i] < bound]
        pool, left = sum([weights[i] for i in movable]), surplus
        for i in movable:
            addition = min(bound - given[i], max(1, left * weights[i] // pool), surplus)
            given[i] = given[i] + addition
            surplus = surplus - addition
    return np.array(given)


def noise(stream_key, shape, scale, bound, cuts=(), kind=jnp.bfloat16):
    values = scale * jax.random.normal(stream_key, shape, jnp.float32)
    if cuts:
        values = values * shard_levels(stream_key, shape, cuts, -0.22, 0.18)
    return jnp.clip(values, -bound, bound).astype(kind)


def setup_inputs(seed: int = 0) -> dict:
    arg_keys = jax.random.split(jax.random.key(seed), 7)
    tokens = noise(arg_keys[0], (TOKENS, D), 1.0, 6.0, ((0, 768),))
    upstream = noise(arg_keys[1], (TOKENS, D), 1.0, 6.0, ((0, 768),))
    task_ids_keys = jax.random.split(jax.random.fold_in(arg_keys[2], 1), TOKENS // TOK_DEV)
    task_ids_turns = jax.random.permutation(jax.random.fold_in(arg_keys[2], 3), TOKENS // TOK_DEV)
    task_ids = jax.vmap(lambda own, number: assign_block(jax.random.fold_in(arg_keys[2], 2), own, number, TOK_DEV, EXPERTS, 1, CAP, 2))(task_ids_keys, task_ids_turns).reshape((TOKENS, 1))
    task_expert = jax.random.permutation(arg_keys[3], EXPERTS).astype(jnp.int32)
    w_in = noise(arg_keys[4], (EXPERTS, D, FF), D ** -0.5, 0.1875, ((0, 48), (2, 16)))
    w_out = noise(arg_keys[5], (EXPERTS, FF, D), FF ** -0.5, 0.09375, ((0, 48), (1, 16)))
    return dict(tokens=tokens, upstream=upstream, task_ids=task_ids, task_expert=task_expert, w_in=w_in, w_out=w_out)


coeff = 0.7978845608028654


def gelu_pair(pre):
    inner = coeff * (pre + 0.044715 * pre * pre * pre)
    tanh_val = jnp.tanh(inner)
    act = 0.5 * pre * (1.0 + tanh_val)
    slope = 0.5 * (1.0 + tanh_val) + 0.5 * pre * (1.0 - tanh_val * tanh_val) * coeff * (1.0 + 3.0 * 0.044715 * pre * pre)
    return act, slope


def reference(tokens, upstream, task_ids, task_expert, w_in, w_out):
    route = task_expert[task_ids[:, 0]].astype(jnp.int32)
    order = jnp.argsort(route, stable=True).astype(jnp.int32)
    hot = (route[:, None] == jnp.arange(EXPERTS, dtype=jnp.int32)[None, :]).astype(jnp.int32)
    counts = jnp.sum(hot, axis=0).astype(jnp.int32)
    offsets = (jnp.cumsum(counts) - counts).astype(jnp.int32)
    most_rows = N_DP * N_EXPERT * CAP
    padded_tokens = jnp.concatenate([tokens, jnp.zeros((1, D), tokens.dtype)], axis=0)
    padded_grads = jnp.concatenate([upstream, jnp.zeros((1, D), upstream.dtype)], axis=0)
    padded_order = jnp.concatenate([order, jnp.zeros((most_rows,), jnp.int32)], axis=0)
    steps_idx = jnp.arange(most_rows, dtype=jnp.int32)

    def one_expert(expert):
        start = offsets[expert]
        picked = lax.dynamic_slice_in_dim(padded_order, start, most_rows, 0)
        index = jnp.where(steps_idx < counts[expert], picked, jnp.int32(TOKENS)).astype(jnp.int32)
        rows = padded_tokens[index]
        grads = padded_grads[index]
        first = w_in[expert]
        second = w_out[expert]
        pre = jnp.dot(rows, first, preferred_element_type=jnp.float32)
        act, slope = gelu_pair(pre)
        act = act.astype(jnp.bfloat16)
        grad_second = jnp.dot(act.T, grads, preferred_element_type=jnp.float32)
        dact = jnp.dot(grads, second.T, preferred_element_type=jnp.float32)
        dpre = (dact * slope).astype(jnp.bfloat16)
        grad_first = jnp.dot(rows.T, dpre, preferred_element_type=jnp.float32)
        total = jnp.zeros((most_rows, D), jnp.float32)
        for block in range(N_DP):
            low = block * FF_DEV
            piece = jnp.dot(dpre[:, low:low + FF_DEV], first[:, low:low + FF_DEV].T, preferred_element_type=jnp.float32)
            total = total + piece.astype(jnp.bfloat16).astype(jnp.float32)
        return total.astype(jnp.bfloat16), index, grad_first, grad_second

    results, indices, grad_in, grad_out = lax.map(one_expert, jnp.arange(EXPERTS, dtype=jnp.int32))
    token_grad = jnp.zeros((TOKENS + 1, D), jnp.bfloat16)
    token_grad = token_grad.at[indices.reshape(-1)].set(results.reshape(-1, D))
    return token_grad[:TOKENS], grad_in, grad_out
```

```python
import jax
import jax.numpy as jnp
from jax import lax
from jax.sharding import Mesh, PartitionSpec as P

coeff = 0.7978845608028654
Y_LO, X, Z, Y_HI, CORE = 4, 4, 12, 2, 2
EXPERT_AXES = ("z", "yh", "c")
LANES = 128


def gelu_pair(pre):
    inner = coeff * (pre + 0.044715 * pre * pre * pre)
    tanh_val = jnp.tanh(inner)
    act = 0.5 * pre * (1.0 + tanh_val)
    slope = 0.5 * (1.0 + tanh_val) + 0.5 * pre * (1.0 - tanh_val * tanh_val) * coeff * (
        1.0 + 3.0 * 0.044715 * pre * pre
    )
    return (act, slope)


def turn(value, amount):
    return lax.ppermute(value, "yl", [(i, (i + amount) % Y_LO) for i in range(Y_LO)])


def body(tokens, upstream, task_ids, task_expert, w_in, w_out):
    rows_dev, width = tokens.shape
    experts = task_expert.shape[0]
    capacity = max(2, (9 * rows_dev // 8 + experts - 1) // experts)
    slots = experts * capacity
    wide_in = lax.all_gather(w_in[0], "x", axis=1, tiled=True)
    wide_out = lax.all_gather(w_out[0], "x", axis=0, tiled=True)

    lanes = jnp.arange(experts, dtype=jnp.int32)
    task_hot = (task_ids == lanes[None, :]).astype(jnp.int32)
    target = jnp.sum(task_hot * task_expert[None, :], axis=1)
    dest_hot = (target[:, None] == lanes[None, :]).astype(jnp.int32)
    before = jnp.cumsum(dest_hot, axis=0) - dest_hot
    rank = jnp.sum(before * dest_hot, axis=1)
    slot = target * capacity + rank
    packer = (jnp.arange(slots, dtype=jnp.int32)[:, None] == slot[None, :]).astype(jnp.bfloat16)

    def pack(value):
        rows = jnp.dot(packer, value, preferred_element_type=jnp.float32).astype(jnp.bfloat16)
        return rows.reshape(experts, capacity * width // LANES, LANES)

    send = jnp.concatenate([pack(tokens), pack(upstream)], axis=1)
    got = lax.all_to_all(send, EXPERT_AXES, split_axis=0, concat_axis=0, tiled=True)
    half = capacity * width // LANES
    own = jnp.concatenate(
        [got[:, :half].reshape(slots, width), got[:, half:].reshape(slots, width)], axis=0
    )
    parts = [own] + [turn(own, k) for k in range(1, Y_LO)]
    rows = jnp.concatenate([part[:slots] for part in parts], axis=0)
    grads = jnp.concatenate([part[slots:] for part in parts], axis=0)

    pre = jnp.dot(rows, wide_in, preferred_element_type=jnp.float32)
    act, slope = gelu_pair(pre)
    act = act.astype(jnp.bfloat16)
    dact = lax.dot_general(
        grads, wide_out, (((1,), (1,)), ((), ())), preferred_element_type=jnp.float32
    )
    dpre = (dact * slope).astype(jnp.bfloat16)
    partial = lax.dot_general(
        dpre, wide_in, (((1,), (1,)), ((), ())), preferred_element_type=jnp.float32
    ).astype(jnp.bfloat16)
    pieces = [partial[k * slots : (k + 1) * slots] for k in range(Y_LO)]
    home = [turn(pieces[k], -k) for k in range(1, Y_LO)]

    part_out = lax.dot_general(
        act, grads, (((0,), (0,)), ((), ())), preferred_element_type=jnp.float32
    ).astype(jnp.bfloat16)
    grad_out = lax.psum_scatter(part_out, "x", scatter_dimension=0, tiled=True)
    part_in = lax.dot_general(
        rows, dpre, (((0,), (0,)), ((), ())), preferred_element_type=jnp.float32
    ).astype(jnp.bfloat16)
    grad_in = lax.psum_scatter(part_in, "x", scatter_dimension=1, tiled=True)

    total = pieces[0].astype(jnp.float32)
    for value in home:
        total = total + value.astype(jnp.float32)
    total = total.astype(jnp.bfloat16).reshape(experts, half, LANES)
    back = lax.all_to_all(total, EXPERT_AXES, split_axis=0, concat_axis=0, tiled=True)
    token_grad = lax.dot_general(
        packer,
        back.reshape(slots, width),
        (((0,), (0,)), ((), ())),
        preferred_element_type=jnp.float32,
    ).astype(jnp.bfloat16)
    return (token_grad, grad_in.astype(jnp.float32)[None], grad_out.astype(jnp.float32)[None])


def solution(mesh):
    fine = Mesh(mesh.devices.reshape(Y_LO, X, Z, Y_HI, CORE), ("yl", "x") + EXPERT_AXES)
    batch = P(("yl", "x") + EXPERT_AXES, None)
    in_weights = P(EXPERT_AXES, None, ("yl", "x"))
    out_weights = P(EXPERT_AXES, ("yl", "x"), None)
    return jax.shard_map(
        body,
        mesh=fine,
        in_specs=(batch, batch, batch, P(), in_weights, out_weights),
        out_specs=(batch, in_weights, out_weights),
        check_vma=False,
    )
```

```python
import jax
import jax.numpy as jnp
from jax import lax
from jax.sharding import Mesh, PartitionSpec as P

coeff = 0.7978845608028654
EXPERT_AXES = ("z", "yh", "c")
EXPERT_SIZES = (12, 2, 2)
DP_AXES = ("yb", "ya", "xh", "xl")
DP_SIZES = (2, 2, 2, 2)
WEIGHT_AXES = ("yb", "xl")
LANES = 128
F32 = jnp.float32
BF16 = jnp.bfloat16


def gelu_pair(pre):
    inner = coeff * (pre + 0.044715 * pre * pre * pre)
    tanh_val = jnp.tanh(inner)
    act = 0.5 * pre * (1.0 + tanh_val)
    slope = 0.5 * (1.0 + tanh_val) + 0.5 * pre * (1.0 - tanh_val * tanh_val) * coeff * (
        1.0 + 3.0 * 0.044715 * pre * pre
    )
    return (act, slope)


def token_y(value):
    return lax.ppermute(value, "ya", [(0, 1), (1, 0)])


def token_x(value):
    return lax.ppermute(value, ("xh", "xl"), [(i, 3 - i) for i in range(4)])


def weight_y(value):
    return lax.ppermute(value, "yb", [(0, 1), (1, 0)])


def weight_x(value):
    return lax.ppermute(value, "xl", [(0, 1), (1, 0)])


def rowdot(left, right):
    return lax.dot_general(left, right, (((0,), (0,)), ((), ())), preferred_element_type=F32)


def lanedot(left, right):
    return lax.dot_general(left, right, (((1,), (1,)), ((), ())), preferred_element_type=F32)


def body(tokens, upstream, task_ids, task_expert, w_in, w_out):
    rows_dev, width = tokens.shape
    experts = task_expert.shape[0]
    capacity = 3
    slots = experts * capacity
    block = w_in.shape[2]
    wide_in = lax.all_gather(w_in[0], WEIGHT_AXES, axis=1, tiled=True)
    wide_out = lax.all_gather(w_out[0], WEIGHT_AXES, axis=0, tiled=True)

    lanes = jnp.arange(experts, dtype=jnp.int32)
    task_hot = (task_ids == lanes[None, :]).astype(jnp.int32)
    target = jnp.sum(task_hot * task_expert[None, :], axis=1)
    dest_hot = (target[:, None] == lanes[None, :]).astype(jnp.int32)
    before = jnp.cumsum(dest_hot, axis=0) - dest_hot
    rank = jnp.sum(before * dest_hot, axis=1)
    slot = target * capacity + rank
    packer = (jnp.arange(slots, dtype=jnp.int32)[:, None] == slot[None, :]).astype(BF16)

    def pack(value):
        rows = jnp.dot(packer, value, preferred_element_type=F32).astype(BF16)
        return rows.reshape(experts, capacity * width // LANES, LANES)

    half = capacity * width // LANES
    send = jnp.concatenate([pack(tokens), pack(upstream)], axis=1)
    got = lax.all_to_all(send, EXPERT_AXES, split_axis=0, concat_axis=0, tiled=True)
    rows0 = got[:, :half].reshape(slots, width)
    grads0 = got[:, half:].reshape(slots, width)
    rows_y = token_y(rows0)
    grads_x = token_x(grads0)
    rows01 = jnp.concatenate([rows0, rows_y], axis=0)
    grads02 = jnp.concatenate([grads0, grads_x], axis=0)
    rows23 = token_x(rows01)
    grads13 = token_y(grads02)
    rows = jnp.concatenate([rows01, rows23], axis=0)
    grads = jnp.concatenate([grads0, grads13[:slots], grads_x, grads13[slots:]], axis=0)

    pre = jnp.dot(rows, wide_in, preferred_element_type=F32)
    act, slope = gelu_pair(pre)
    act = act.astype(BF16)
    dpre = (lanedot(grads, wide_out) * slope).astype(BF16)
    part = lanedot(dpre, wide_in).astype(BF16)
    part_out = rowdot(act, grads).astype(BF16)
    grad_out = lax.psum_scatter(part_out, WEIGHT_AXES, scatter_dimension=0, tiled=True)

    cut = width // 2
    p0, p1, p2, p3 = [part[i * slots : (i + 1) * slots] for i in range(4)]
    left = token_y(jnp.concatenate([p1[:, :cut], p3[:, :cut]], axis=0))
    right = token_x(jnp.concatenate([p2[:, cut:], p3[:, cut:]], axis=0))
    rows_later, dpre_later, _ = lax.optimization_barrier((rows, dpre, part))
    part_in = rowdot(rows_later, dpre_later).astype(BF16)
    left_own = p0[:, :cut].astype(F32) + left[:slots].astype(F32)
    left_send = (p2[:, :cut].astype(F32) + left[slots:].astype(F32)).astype(BF16)
    right_own = p0[:, cut:].astype(F32) + right[:slots].astype(F32)
    right_send = (p1[:, cut:].astype(F32) + right[slots:].astype(F32)).astype(BF16)
    left_total = left_own + token_x(left_send).astype(F32)
    right_total = right_own + token_y(right_send).astype(F32)
    total = jnp.concatenate([left_total, right_total], axis=1).astype(BF16)

    yb, xl = lax.axis_index("yb"), lax.axis_index("xl")
    parts = part_in.reshape(width, 2, 2, block)
    mine = lax.dynamic_index_in_dim(parts, xl, 2, keepdims=False)
    theirs = lax.dynamic_index_in_dim(parts, 1 - xl, 2, keepdims=False)
    pair = mine.astype(F32) + weight_x(theirs).astype(F32)
    keep = lax.dynamic_index_in_dim(pair, yb, 1, keepdims=False)
    give = lax.dynamic_index_in_dim(pair, 1 - yb, 1, keepdims=False).astype(BF16)
    grad_in = keep + weight_y(give).astype(F32)

    back = lax.all_to_all(
        total.reshape(experts, half, LANES), EXPERT_AXES, split_axis=0, concat_axis=0, tiled=True
    )
    token_grad = rowdot(packer, back.reshape(slots, width)).astype(BF16)
    return (token_grad, grad_in[None], grad_out.astype(F32)[None])


def solution(mesh):
    fine = Mesh(mesh.devices.reshape(DP_SIZES + EXPERT_SIZES), DP_AXES + EXPERT_AXES)
    batch = P(DP_AXES + EXPERT_AXES, None)
    in_weights = P(EXPERT_AXES, None, DP_AXES)
    out_weights = P(EXPERT_AXES, DP_AXES, None)
    return jax.shard_map(
        body,
        mesh=fine,
        in_specs=(batch, batch, batch, P(), in_weights, out_weights),
        out_specs=(batch, in_weights, out_weights),
        check_vma=False,
    )
```

```python
import jax
import jax.numpy as jnp
from jax import lax
from jax.sharding import Mesh, PartitionSpec as P

coeff = 0.7978845608028654
Y_LO, X, Z, Y_HI, CORE = 4, 4, 12, 2, 2
EXPERT_AXES = ("z", "yh", "c")
LANES = 128


def gelu_pair(pre):
    inner = coeff * (pre + 0.044715 * pre * pre * pre)
    tanh_val = jnp.tanh(inner)
    act = 0.5 * pre * (1.0 + tanh_val)
    slope = 0.5 * (1.0 + tanh_val) + 0.5 * pre * (1.0 - tanh_val * tanh_val) * coeff * (
        1.0 + 3.0 * 0.044715 * pre * pre
    )
    return (act, slope)


def turn(value, axis, amount):
    size = lax.axis_size(axis)
    return lax.ppermute(value, axis, [(i, (i + amount) % size) for i in range(size)])


def rowdot(left, right):
    return lax.dot_general(
        left, right, (((0,), (0,)), ((), ())), preferred_element_type=jnp.float32
    )


def body(tokens, upstream, task_ids, task_expert, w_in, w_out):
    rows_dev, width = tokens.shape
    experts = task_expert.shape[0]
    capacity = max(2, (9 * rows_dev // 8 + experts - 1) // experts)
    slots = experts * capacity
    wide_in = lax.all_gather(w_in[0], "x", axis=1, tiled=True)
    wide_out = lax.all_gather(w_out[0], "x", axis=0, tiled=True)

    lanes = jnp.arange(experts, dtype=jnp.int32)
    task_hot = (task_ids == lanes[None, :]).astype(jnp.int32)
    target = jnp.sum(task_hot * task_expert[None, :], axis=1)
    dest_hot = (target[:, None] == lanes[None, :]).astype(jnp.int32)
    before = jnp.cumsum(dest_hot, axis=0) - dest_hot
    rank = jnp.sum(before * dest_hot, axis=1)
    slot = target * capacity + rank
    packer = (jnp.arange(slots, dtype=jnp.int32)[:, None] == slot[None, :]).astype(jnp.bfloat16)

    def pack(value):
        rows = jnp.dot(packer, value, preferred_element_type=jnp.float32).astype(jnp.bfloat16)
        return rows.reshape(experts, capacity * width // LANES, LANES)

    send = jnp.concatenate([pack(tokens), pack(upstream)], axis=1)
    got = lax.all_to_all(send, EXPERT_AXES, split_axis=0, concat_axis=0, tiled=True)
    half = capacity * width // LANES
    own = jnp.concatenate(
        [got[:, :half].reshape(slots, width), got[:, half:].reshape(slots, width)], axis=0
    )
    third = 2 * slots // 3
    pieces = [
        lax.all_gather(own[k * third : (k + 1) * third], "yl", axis=0, tiled=False)
        for k in range(3)
    ]
    whole = jnp.concatenate(pieces, axis=1)
    rows = whole[:, :slots].reshape(Y_LO * slots, width)
    grads = whole[:, slots:].reshape(Y_LO * slots, width)

    pre = jnp.dot(rows, wide_in, preferred_element_type=jnp.float32)
    act, slope = gelu_pair(pre)
    act = act.astype(jnp.bfloat16)
    dact = lax.dot_general(
        grads, wide_out, (((1,), (1,)), ((), ())), preferred_element_type=jnp.float32
    )
    dpre = (dact * slope).astype(jnp.bfloat16)
    partial = lax.dot_general(
        dpre, wide_in, (((1,), (1,)), ((), ())), preferred_element_type=jnp.float32
    ).astype(jnp.bfloat16)
    y = lax.axis_index("yl")
    owners = [lax.rem(y + k, Y_LO) for k in range(Y_LO)]
    pieces = [lax.dynamic_slice_in_dim(partial, o * slots, slots, 0) for o in owners]
    home = [turn(pieces[k], "yl", k) for k in (1, 2, 3)]
    act, grads, rows, dpre, _ = lax.optimization_barrier((act, grads, rows, dpre, partial))

    part_out = rowdot(act, grads).astype(jnp.bfloat16)
    grad_out = lax.psum_scatter(part_out, "x", scatter_dimension=0, tiled=True)
    x = lax.axis_index("x")
    block = w_in.shape[2]
    grad_in = None
    for k in (1, 3, 2, 0):
        start = lax.rem(x + k, X) * block
        part = rowdot(rows, lax.dynamic_slice_in_dim(dpre, start, block, 1))
        if k:
            part = turn(part.astype(jnp.bfloat16), "x", k).astype(jnp.float32)
        grad_in = part if grad_in is None else grad_in + part

    total = pieces[0].astype(jnp.float32)
    for value in home:
        total = total + value.astype(jnp.float32)
    total = total.astype(jnp.bfloat16).reshape(experts, half, LANES)
    back = lax.all_to_all(total, EXPERT_AXES, split_axis=0, concat_axis=0, tiled=True)
    token_grad = lax.dot_general(
        packer,
        back.reshape(slots, width),
        (((0,), (0,)), ((), ())),
        preferred_element_type=jnp.float32,
    ).astype(jnp.bfloat16)
    return (token_grad, grad_in[None], grad_out.astype(jnp.float32)[None])


def solution(mesh):
    fine = Mesh(mesh.devices.reshape(Y_LO, X, Z, Y_HI, CORE), ("yl", "x") + EXPERT_AXES)
    batch = P(("yl", "x") + EXPERT_AXES, None)
    in_weights = P(EXPERT_AXES, None, ("yl", "x"))
    out_weights = P(EXPERT_AXES, ("yl", "x"), None)
    return jax.shard_map(
        body,
        mesh=fine,
        in_specs=(batch, batch, batch, P(), in_weights, out_weights),
        out_specs=(batch, in_weights, out_weights),
        check_vma=False,
    )
```

```python
import jax
import jax.numpy as jnp
from jax import lax
from jax.experimental import pallas as pl
from jax.experimental.pallas import tpu as pltpu
from jax.sharding import Mesh, PartitionSpec as P

coeff = 0.7978845608028654
Y_LO, X, Z, Y_HI, CORE = 4, 4, 12, 2, 2
EXPERT_AXES = ("z", "yh", "c")
LANES = 128


def gelu_pair(pre):
    inner = coeff * (pre + 0.044715 * pre * pre * pre)
    tanh_val = jnp.tanh(inner)
    act = 0.5 * pre * (1.0 + tanh_val)
    slope = 0.5 * (1.0 + tanh_val) + 0.5 * pre * (1.0 - tanh_val * tanh_val) * coeff * (
        1.0 + 3.0 * 0.044715 * pre * pre
    )
    return (act, slope)


def turn(value, axis, amount):
    size = lax.axis_size(axis)
    return lax.ppermute(value, axis, [(i, (i + amount) % size) for i in range(size)])


def rowdot(left, right):
    return lax.dot_general(
        left, right, (((0,), (0,)), ((), ())), preferred_element_type=jnp.float32
    )


def lanedot(left, right):
    return lax.dot_general(
        left, right, (((1,), (1,)), ((), ())), preferred_element_type=jnp.float32
    )


def expert_kernel(place, c0, c1, c2, win_in, wout_in, *refs):
    go_out, rows_out = refs[:2]
    dpre_out, part_out = refs[2], refs[3:7]
    rows, grads, win, wout, go, dpre, part, sems = refs[7:]
    slots = part.shape[0] // Y_LO
    step = win.shape[1] // X
    first = c0.shape[1]
    rest = slots - first
    used = []

    def copy(src, dst):
        used.append(pltpu.make_async_copy(src, dst, sems.at[len(used)]))
        used[-1].start()
        return used[-1]

    def near(axis, size, amount):
        return lax.rem(place[axis] + amount, size)

    row_loads, grad_loads, win_loads, wout_loads = [], [], [], []
    for k in range(Y_LO):
        src = near(0, Y_LO, k)
        base = k * slots
        row_loads.append(copy(c0.at[src], rows.at[pl.ds(base, first)]))
        row_loads.append(copy(c1.at[src, pl.ds(0, rest)], rows.at[pl.ds(base + first, rest)]))
    for k in range(X):
        src = pl.ds(pl.multiple_of(near(1, X, k) * step, step), step)
        win_loads.append(copy(win_in.at[:, src], win.at[:, pl.ds(k * step, step)]))
    for k in range(Y_LO):
        src = near(0, Y_LO, k)
        base = k * slots
        grad_loads.append(copy(c1.at[src, pl.ds(rest, rest)], grads.at[pl.ds(base, rest)]))
        grad_loads.append(copy(c2.at[src], grads.at[pl.ds(base + rest, first)]))
    for k in range(X):
        src = pl.ds(pl.multiple_of(near(1, X, k) * step, step), step)
        wout_loads.append(copy(wout_in.at[src], wout.at[pl.ds(k * step, step)]))
    for load in row_loads:
        load.wait()
    stores = [copy(rows, rows_out)]
    for k in range(X):
        cols = pl.ds(k * step, step)
        win_loads[k].wait()
        pre = jnp.dot(rows[...], win[:, cols], preferred_element_type=jnp.float32)
        if k == 0:
            for load in grad_loads:
                load.wait()
        wout_loads[k].wait()
        dact = lanedot(grads[...], wout[cols, :])
        act, slope = gelu_pair(pre)
        dpre[:, cols] = (dact * slope).astype(jnp.bfloat16)
        go[cols, :] = rowdot(act.astype(jnp.bfloat16), grads[...]).astype(jnp.bfloat16)
        dst = pl.ds(pl.multiple_of(near(1, X, k) * step, step), step)
        stores.append(copy(go.at[cols, :], go_out.at[dst]))
    stores.append(copy(dpre, dpre_out))
    part[...] = lanedot(dpre[...], win[...]).astype(jnp.bfloat16)
    for k in range(Y_LO):
        stores.append(copy(part.at[pl.ds(k * slots, slots)], part_out[k]))
    for store in stores:
        store.wait()


def expert_products(place, pieces, win, wout):
    _, first, width = pieces[0].shape
    hidden = win.shape[1]
    slots = first * 3 // 2
    count = slots * Y_LO
    shapes = [(hidden, width), (count, width)]
    shapes += [(count, hidden)] + [(slots, width)] * Y_LO
    scratch = [(count, width)] * 2 + [(width, hidden), (hidden, width)]
    scratch += [(hidden, width), (count, hidden), (count, width)]
    anywhere = pl.BlockSpec(memory_space=pl.ANY)
    main = pl.BlockSpec(memory_space=pltpu.HBM)
    return pl.pallas_call(
        expert_kernel,
        out_shape=[jax.ShapeDtypeStruct(shape, jnp.bfloat16) for shape in shapes],
        in_specs=[pl.BlockSpec(memory_space=pltpu.SMEM)] + [anywhere] * 3 + [main] * 2,
        out_specs=[main] * (3 + Y_LO),
        scratch_shapes=[pltpu.VMEM(shape, jnp.bfloat16) for shape in scratch]
        + [pltpu.SemaphoreType.DMA((4 * Y_LO + 2 * X + 1 + X + 1 + Y_LO,))],
        compiler_params=pltpu.CompilerParams(vmem_limit_bytes=58 * 1024 * 1024),
        cost_estimate=pl.CostEstimate(
            flops=8 * count * width * hidden, bytes_accessed=11 << 20, transcendentals=count * hidden
        ),
    )(place, *pieces, win, wout)


def body(tokens, upstream, task_ids, task_expert, w_in, w_out):
    rows_dev, width = tokens.shape
    experts = task_expert.shape[0]
    capacity = max(2, (9 * rows_dev // 8 + experts - 1) // experts)
    slots = experts * capacity
    wide_in = lax.all_gather(w_in[0], "x", axis=1, tiled=True)
    wide_out = lax.all_gather(w_out[0], "x", axis=0, tiled=True)

    lanes = jnp.arange(experts, dtype=jnp.int32)
    task_hot = (task_ids == lanes[None, :]).astype(jnp.int32)
    target = jnp.sum(task_hot * task_expert[None, :], axis=1)
    dest_hot = (target[:, None] == lanes[None, :]).astype(jnp.int32)
    before = jnp.cumsum(dest_hot, axis=0) - dest_hot
    rank = jnp.sum(before * dest_hot, axis=1)
    slot = target * capacity + rank
    packer = (jnp.arange(slots, dtype=jnp.int32)[:, None] == slot[None, :]).astype(jnp.bfloat16)

    def pack(value):
        rows = jnp.dot(packer, value, preferred_element_type=jnp.float32).astype(jnp.bfloat16)
        return rows.reshape(experts, capacity * width // LANES, LANES)

    send = jnp.concatenate([pack(tokens), pack(upstream)], axis=1)
    got = lax.all_to_all(send, EXPERT_AXES, split_axis=0, concat_axis=0, tiled=True)
    half = capacity * width // LANES
    own = jnp.concatenate(
        [got[:, :half].reshape(slots, width), got[:, half:].reshape(slots, width)], axis=0
    )
    third = 2 * slots // 3
    pieces = [
        lax.all_gather(own[k * third : (k + 1) * third], "yl", axis=0, tiled=False)
        for k in range(3)
    ]
    place = jnp.stack([lax.axis_index("yl"), lax.axis_index("x")]).astype(jnp.int32)
    products = expert_products(place, pieces, wide_in, wide_out)
    part_out, rows = products[:2]
    dpre, pieces = products[2], products[3:]
    grad_out = lax.psum_scatter(part_out, "x", scatter_dimension=0, tiled=True)
    home = [turn(pieces[k], "yl", k) for k in (1, 2, 3)]

    block = w_in.shape[2]

    def own_block(k):
        return rowdot(rows, dpre[:, k * block : (k + 1) * block])

    def sent(k):
        return turn(own_block(k).astype(jnp.bfloat16), "x", k)

    one, three, two = sent(1), sent(3), sent(2)
    rows, one, three = lax.optimization_barrier((rows, one, three))
    near_sum = own_block(0) + one.astype(jnp.float32) + three.astype(jnp.float32)
    near_sum, two = lax.optimization_barrier((near_sum, two))
    grad_in = near_sum + two.astype(jnp.float32)

    total = pieces[0].astype(jnp.float32)
    for value in home:
        total = total + value.astype(jnp.float32)
    total = total.astype(jnp.bfloat16).reshape(experts, half, LANES)
    back = lax.all_to_all(total, EXPERT_AXES, split_axis=0, concat_axis=0, tiled=True)
    token_grad = lax.dot_general(
        packer,
        back.reshape(slots, width),
        (((0,), (0,)), ((), ())),
        preferred_element_type=jnp.float32,
    ).astype(jnp.bfloat16)
    return (token_grad, grad_in[None], grad_out.astype(jnp.float32)[None])


def solution(mesh):
    fine = Mesh(mesh.devices.reshape(Y_LO, X, Z, Y_HI, CORE), ("yl", "x") + EXPERT_AXES)
    batch = P(("yl", "x") + EXPERT_AXES, None)
    in_weights = P(EXPERT_AXES, None, ("yl", "x"))
    out_weights = P(EXPERT_AXES, ("yl", "x"), None)
    return jax.shard_map(
        body,
        mesh=fine,
        in_specs=(batch, batch, batch, P(), in_weights, out_weights),
        out_specs=(batch, in_weights, out_weights),
        check_vma=False,
    )
```

```python
import jax
import jax.numpy as jnp
from jax import lax
from jax.experimental import pallas as pl
from jax.experimental.pallas import tpu as pltpu
from jax.sharding import Mesh, PartitionSpec as P

coeff = 0.7978845608028654
Y_LO, X, Z, Y_HI, CORE = 4, 4, 12, 2, 2
EXPERT_AXES = ("z", "yh", "c")
LANES = 128


def gelu_pair(pre):
    square = pre * pre
    tanh_val = jnp.tanh(pre * (coeff + (coeff * 0.044715) * square))
    share = 0.5 + 0.5 * tanh_val
    act = pre * share
    slope = share + (0.5 * pre) * (1.0 - tanh_val * tanh_val) * (
        coeff + (coeff * 3.0 * 0.044715) * square
    )
    return (act, slope)


def turn(value, axis, amount):
    size = lax.axis_size(axis)
    return lax.ppermute(value, axis, [(i, (i + amount) % size) for i in range(size)])


def rowdot(left, right):
    return lax.dot_general(
        left, right, (((0,), (0,)), ((), ())), preferred_element_type=jnp.float32
    )


def lanedot(left, right):
    return lax.dot_general(
        left, right, (((1,), (1,)), ((), ())), preferred_element_type=jnp.float32
    )


def expert_kernel(place, c0, c1, c2, win_in, wout_in, *refs):
    go_out, rows_out = refs[:2]
    dpre_out, part_out = refs[2], refs[3:7]
    rows, grads, win, wout, go, dpre, part, sems = refs[7:]
    slots = part.shape[0] // Y_LO
    step = win.shape[1] // X
    first = c0.shape[1]
    rest = slots - first
    used = []

    def copy(src, dst):
        used.append(pltpu.make_async_copy(src, dst, sems.at[len(used)]))
        used[-1].start()
        return used[-1]

    def near(axis, size, amount):
        return lax.rem(place[axis] + amount, size)

    row_loads, grad_loads, win_loads, wout_loads = [], [], [], []

    def load_weights(k):
        src = pl.ds(pl.multiple_of(near(1, X, k) * step, step), step)
        cols = pl.ds(k * step, step)
        win_loads.append(copy(win_in.at[near(1, X, k)], win.at[:, cols]))
        return lambda: wout_loads.append(copy(wout_in.at[src], wout.at[cols]))

    later = load_weights(0)
    for k in range(Y_LO):
        src = near(0, Y_LO, k)
        base = k * slots
        row_loads.append(copy(c0.at[src], rows.at[pl.ds(base, first)]))
        row_loads.append(copy(c1.at[src, pl.ds(0, rest)], rows.at[pl.ds(base + first, rest)]))
    after = [later] + [load_weights(k) for k in range(1, X)]
    for k in range(Y_LO):
        src = near(0, Y_LO, k)
        base = k * slots
        grad_loads.append(copy(c1.at[src, pl.ds(rest, rest)], grads.at[pl.ds(base, rest)]))
        grad_loads.append(copy(c2.at[src], grads.at[pl.ds(base + rest, first)]))
    for later in after:
        later()
    stores = []
    win_loads[0].wait()
    for load in row_loads:
        load.wait()
    pres = []
    for k in range(X):
        cols = pl.ds(k * step, step)
        if k:
            win_loads[k].wait()
        pres.append(jnp.dot(rows[...], win[:, cols], preferred_element_type=jnp.float32))
    for load in grad_loads:
        load.wait()
    for k in range(X):
        cols = pl.ds(k * step, step)
        pre = pres[k]
        wout_loads[k].wait()
        dact = lanedot(grads[...], wout[cols, :])
        act, slope = gelu_pair(pre)
        dpre[:, cols] = (dact * slope).astype(jnp.bfloat16)
        go[cols, :] = rowdot(act.astype(jnp.bfloat16), grads[...]).astype(jnp.bfloat16)
        dst = pl.ds(pl.multiple_of(near(1, X, k) * step, step), step)
        stores.append(copy(go.at[cols, :], go_out.at[dst]))
    stores.append(copy(rows, rows_out))
    stores.append(copy(dpre, dpre_out))
    part[...] = lanedot(dpre[...], win[...]).astype(jnp.bfloat16)
    for k in range(Y_LO):
        stores.append(copy(part.at[pl.ds(k * slots, slots)], part_out[k]))
    for store in stores:
        store.wait()


def expert_products(place, pieces, win, wout):
    _, first, width = pieces[0].shape
    hidden = wout.shape[0]
    slots = first * 3 // 2
    count = slots * Y_LO
    shapes = [(hidden, width), (count, width)]
    shapes += [(count, hidden)] + [(slots, width)] * Y_LO
    scratch = [(count, width)] * 2 + [(width, hidden), (hidden, width)]
    scratch += [(hidden, width), (count, hidden), (count, width)]
    anywhere = pl.BlockSpec(memory_space=pl.ANY)
    main = pl.BlockSpec(memory_space=pltpu.HBM)
    return pl.pallas_call(
        expert_kernel,
        out_shape=[jax.ShapeDtypeStruct(shape, jnp.bfloat16) for shape in shapes],
        in_specs=[pl.BlockSpec(memory_space=pltpu.SMEM)] + [anywhere] * 3 + [main] * 2,
        out_specs=[main] * (3 + Y_LO),
        scratch_shapes=[pltpu.VMEM(shape, jnp.bfloat16) for shape in scratch]
        + [pltpu.SemaphoreType.DMA((4 * Y_LO + 2 * X + 1 + X + 1 + Y_LO,))],
        compiler_params=pltpu.CompilerParams(vmem_limit_bytes=50 * 1024 * 1024),
        cost_estimate=pl.CostEstimate(
            flops=8 * count * width * hidden, bytes_accessed=11 << 20, transcendentals=count * hidden
        ),
    )(place, *pieces, win, wout)


def body(tokens, upstream, task_ids, task_expert, w_in, w_out):
    rows_dev, width = tokens.shape
    experts = task_expert.shape[0]
    capacity = max(2, (9 * rows_dev // 8 + experts - 1) // experts)
    slots = experts * capacity
    wide_in = lax.all_gather(w_in[0], "x", axis=0, tiled=False)
    wide_out = lax.all_gather(w_out[0], "x", axis=0, tiled=True)

    lanes = jnp.arange(experts, dtype=jnp.int32)
    task_hot = (task_ids == lanes[None, :]).astype(jnp.int32)
    target = jnp.sum(task_hot * task_expert[None, :], axis=1)
    dest_hot = (target[:, None] == lanes[None, :]).astype(jnp.int32)
    before = jnp.cumsum(dest_hot, axis=0) - dest_hot
    rank = jnp.sum(before * dest_hot, axis=1)
    slot = target * capacity + rank
    packer = (jnp.arange(slots, dtype=jnp.int32)[:, None] == slot[None, :]).astype(jnp.bfloat16)

    def pack(value):
        rows = jnp.dot(packer, value, preferred_element_type=jnp.float32).astype(jnp.bfloat16)
        return rows.reshape(experts, capacity * width // LANES, LANES)

    send = jnp.concatenate([pack(tokens), pack(upstream)], axis=1)
    got = lax.all_to_all(send, EXPERT_AXES, split_axis=0, concat_axis=0, tiled=True)
    half = capacity * width // LANES
    own = jnp.concatenate(
        [got[:, :half].reshape(slots, width), got[:, half:].reshape(slots, width)], axis=0
    )
    third = 2 * slots // 3
    pieces = [
        lax.all_gather(own[k * third : (k + 1) * third], "yl", axis=0, tiled=False)
        for k in range(3)
    ]
    place = jnp.stack([lax.axis_index("yl"), lax.axis_index("x")]).astype(jnp.int32)
    products = expert_products(place, pieces, wide_in, wide_out)
    part_out, rows = products[:2]
    dpre, pieces = products[2], products[3:]
    grad_out = lax.psum_scatter(part_out, "x", scatter_dimension=0, tiled=True)
    home = [turn(pieces[k], "yl", k) for k in (1, 2, 3)]

    block = w_in.shape[2]

    def own_block(k):
        return rowdot(rows, dpre[:, k * block : (k + 1) * block])

    def sent(k):
        return turn(own_block(k).astype(jnp.bfloat16), "x", k)

    one, three, two = sent(1), sent(3), sent(2)
    rows, one, three = lax.optimization_barrier((rows, one, three))
    near_sum = own_block(0) + one.astype(jnp.float32) + three.astype(jnp.float32)
    near_sum, two = lax.optimization_barrier((near_sum, two))
    grad_in = near_sum + two.astype(jnp.float32)

    total = pieces[0].astype(jnp.float32)
    for value in home:
        total = total + value.astype(jnp.float32)
    total = total.astype(jnp.bfloat16).reshape(experts, half, LANES)
    back = lax.all_to_all(total, EXPERT_AXES, split_axis=0, concat_axis=0, tiled=True)
    token_grad = lax.dot_general(
        packer,
        back.reshape(slots, width),
        (((0,), (0,)), ((), ())),
        preferred_element_type=jnp.float32,
    ).astype(jnp.bfloat16)
    return (token_grad, grad_in[None], grad_out.astype(jnp.float32)[None])


def solution(mesh):
    fine = Mesh(mesh.devices.reshape(Y_LO, X, Z, Y_HI, CORE), ("yl", "x") + EXPERT_AXES)
    batch = P(("yl", "x") + EXPERT_AXES, None)
    in_weights = P(EXPERT_AXES, None, ("yl", "x"))
    out_weights = P(EXPERT_AXES, ("yl", "x"), None)
    return jax.shard_map(
        body,
        mesh=fine,
        in_specs=(batch, batch, batch, P(), in_weights, out_weights),
        out_specs=(batch, in_weights, out_weights),
        check_vma=False,
    )
```

```python
import jax
import jax.numpy as jnp
from jax import lax
from jax.experimental import pallas as pl
from jax.experimental.pallas import tpu as pltpu
from jax.sharding import Mesh, PartitionSpec as P

coeff = 0.7978845608028654
Y_LO, X, Z, Y_HI, CORE = 4, 4, 12, 2, 2
EXPERT_AXES = ("z", "yh", "c")
LANES = 128


def gelu_pair(pre):
    square = pre * pre
    tanh_val = jnp.tanh(pre * (coeff + (coeff * 0.044715) * square))
    share = 0.5 + 0.5 * tanh_val
    act = pre * share
    slope = share + (0.5 * pre) * (1.0 - tanh_val * tanh_val) * (
        coeff + (coeff * 3.0 * 0.044715) * square
    )
    return (act, slope)


def turn(value, axis, amount):
    size = lax.axis_size(axis)
    return lax.ppermute(value, axis, [(i, (i + amount) % size) for i in range(size)])


def rowdot(left, right):
    return lax.dot_general(
        left, right, (((0,), (0,)), ((), ())), preferred_element_type=jnp.float32
    )


def lanedot(left, right):
    return lax.dot_general(
        left, right, (((1,), (1,)), ((), ())), preferred_element_type=jnp.float32
    )


def expert_kernel(place, c0, c1, c2, win_in, wout_in, *refs):
    go_out, rows_out = refs[:2]
    dpre_out, part_out = refs[2], refs[3:7]
    rows, grads, win, wout, go, dpre, part, sems = refs[7:]
    slots = part.shape[0] // Y_LO
    step = win.shape[1] // X
    first = c0.shape[1]
    rest = slots - first
    used = []

    def copy(src, dst):
        used.append(pltpu.make_async_copy(src, dst, sems.at[len(used)]))
        used[-1].start()
        return used[-1]

    def near(axis, size, amount):
        return lax.rem(place[axis] + amount, size)

    row_loads, grad_loads, win_loads, wout_loads = [], [], [], []

    def load_weights(k):
        src = pl.ds(pl.multiple_of(near(1, X, k) * step, step), step)
        cols = pl.ds(k * step, step)
        win_loads.append(copy(win_in.at[near(1, X, k)], win.at[:, cols]))
        return lambda: wout_loads.append(copy(wout_in.at[src], wout.at[cols]))

    later = load_weights(0)
    for k in range(Y_LO):
        src = near(0, Y_LO, k)
        base = k * slots
        row_loads.append(copy(c0.at[src], rows.at[pl.ds(base, first)]))
        row_loads.append(copy(c1.at[src, pl.ds(0, rest)], rows.at[pl.ds(base + first, rest)]))
    after = [later] + [load_weights(k) for k in range(1, X)]
    for k in range(Y_LO):
        src = near(0, Y_LO, k)
        base = k * slots
        grad_loads.append(copy(c1.at[src, pl.ds(rest, rest)], grads.at[pl.ds(base, rest)]))
        grad_loads.append(copy(c2.at[src], grads.at[pl.ds(base + rest, first)]))
    for later in after:
        later()
    stores = []
    win_loads[0].wait()
    for load in row_loads:
        load.wait()
    pres = []
    for k in range(X):
        cols = pl.ds(k * step, step)
        if k:
            win_loads[k].wait()
        pres.append(jnp.dot(rows[...], win[:, cols], preferred_element_type=jnp.float32))
    for load in grad_loads + wout_loads:
        load.wait()
    dact = lanedot(grads[...], wout[...])
    for k in range(X):
        cols = pl.ds(k * step, step)
        act, slope = gelu_pair(pres[k])
        dpre[:, cols] = (dact[:, k * step : (k + 1) * step] * slope).astype(jnp.bfloat16)
        go[cols, :] = rowdot(act.astype(jnp.bfloat16), grads[...]).astype(jnp.bfloat16)
        dst = pl.ds(pl.multiple_of(near(1, X, k) * step, step), step)
        stores.append(copy(go.at[cols, :], go_out.at[dst]))
    stores.append(copy(rows, rows_out))
    stores.append(copy(dpre, dpre_out))
    part[...] = lanedot(dpre[...], win[...]).astype(jnp.bfloat16)
    for k in range(Y_LO):
        stores.append(copy(part.at[pl.ds(k * slots, slots)], part_out[k]))
    for store in stores:
        store.wait()


def expert_products(place, pieces, win, wout):
    _, first, width = pieces[0].shape
    hidden = wout.shape[0]
    slots = first * 3 // 2
    count = slots * Y_LO
    shapes = [(hidden, width), (count, width)]
    shapes += [(count, hidden)] + [(slots, width)] * Y_LO
    scratch = [(count, width)] * 2 + [(width, hidden), (hidden, width)]
    scratch += [(hidden, width), (count, hidden), (count, width)]
    anywhere = pl.BlockSpec(memory_space=pl.ANY)
    main = pl.BlockSpec(memory_space=pltpu.HBM)
    return pl.pallas_call(
        expert_kernel,
        out_shape=[jax.ShapeDtypeStruct(shape, jnp.bfloat16) for shape in shapes],
        in_specs=[pl.BlockSpec(memory_space=pltpu.SMEM)] + [anywhere] * 3 + [main] * 2,
        out_specs=[main] * (3 + Y_LO),
        scratch_shapes=[pltpu.VMEM(shape, jnp.bfloat16) for shape in scratch]
        + [pltpu.SemaphoreType.DMA((4 * Y_LO + 2 * X + 1 + X + 1 + Y_LO,))],
        compiler_params=pltpu.CompilerParams(vmem_limit_bytes=50 * 1024 * 1024),
        cost_estimate=pl.CostEstimate(
            flops=8 * count * width * hidden, bytes_accessed=11 << 20, transcendentals=count * hidden
        ),
    )(place, *pieces, win, wout)


def body(tokens, upstream, task_ids, task_expert, w_in, w_out):
    rows_dev, width = tokens.shape
    experts = task_expert.shape[0]
    capacity = max(2, (9 * rows_dev // 8 + experts - 1) // experts)
    slots = experts * capacity
    wide_in = lax.all_gather(w_in[0], "x", axis=0, tiled=False)
    wide_out = lax.all_gather(w_out[0], "x", axis=0, tiled=True)

    lanes = jnp.arange(experts, dtype=jnp.int32)
    task_hot = (task_ids == lanes[None, :]).astype(jnp.int32)
    target = jnp.sum(task_hot * task_expert[None, :], axis=1)
    dest_hot = (target[:, None] == lanes[None, :]).astype(jnp.int32)
    before = jnp.cumsum(dest_hot, axis=0) - dest_hot
    rank = jnp.sum(before * dest_hot, axis=1)
    slot = target * capacity + rank
    packer = (jnp.arange(slots, dtype=jnp.int32)[:, None] == slot[None, :]).astype(jnp.bfloat16)

    def pack(value):
        rows = jnp.dot(packer, value, preferred_element_type=jnp.float32).astype(jnp.bfloat16)
        return rows.reshape(experts, capacity * width // LANES, LANES)

    half = capacity * width // LANES

    def exchange(value):
        return lax.all_to_all(value, EXPERT_AXES, split_axis=0, concat_axis=0, tiled=True)

    def over_y(value):
        return lax.all_gather(value, "yl", axis=0, tiled=False)

    first = 2 * slots // 3
    row = exchange(pack(tokens)).reshape(slots, width)
    grad_packed, row = lax.optimization_barrier((pack(upstream), row))
    pieces = [over_y(row[:first])]
    grad, pieces[0] = lax.optimization_barrier((exchange(grad_packed), pieces[0]))
    grad = grad.reshape(slots, width)
    pieces.append(over_y(jnp.concatenate([row[first:], grad[: slots - first]], axis=0)))
    pieces.append(over_y(grad[slots - first :]))

    place = jnp.stack([lax.axis_index("yl"), lax.axis_index("x")]).astype(jnp.int32)
    products = expert_products(place, pieces, wide_in, wide_out)
    part_out, rows = products[:2]
    dpre, pieces = products[2], products[3:]
    grad_out = lax.psum_scatter(part_out, "x", scatter_dimension=0, tiled=True)
    home = [turn(pieces[k], "yl", k) for k in (1, 2, 3)]

    block = w_in.shape[2]

    def own_block(k):
        return rowdot(rows, dpre[:, k * block : (k + 1) * block])

    def sent(k):
        return turn(own_block(k).astype(jnp.bfloat16), "x", k)

    one, three, two = sent(1), sent(3), sent(2)
    rows, one, three = lax.optimization_barrier((rows, one, three))
    near_sum = own_block(0) + one.astype(jnp.float32) + three.astype(jnp.float32)
    near_sum, two = lax.optimization_barrier((near_sum, two))
    grad_in = near_sum + two.astype(jnp.float32)

    total = pieces[0].astype(jnp.float32)
    for value in home:
        total = total + value.astype(jnp.float32)
    total = total.astype(jnp.bfloat16).reshape(experts, half, LANES)
    back = lax.all_to_all(total, EXPERT_AXES, split_axis=0, concat_axis=0, tiled=True)
    token_grad = lax.dot_general(
        packer,
        back.reshape(slots, width),
        (((0,), (0,)), ((), ())),
        preferred_element_type=jnp.float32,
    ).astype(jnp.bfloat16)
    return (token_grad, grad_in[None], grad_out.astype(jnp.float32)[None])


def solution(mesh):
    fine = Mesh(mesh.devices.reshape(Y_LO, X, Z, Y_HI, CORE), ("yl", "x") + EXPERT_AXES)
    batch = P(("yl", "x") + EXPERT_AXES, None)
    in_weights = P(EXPERT_AXES, None, ("yl", "x"))
    out_weights = P(EXPERT_AXES, ("yl", "x"), None)
    return jax.shard_map(
        body,
        mesh=fine,
        in_specs=(batch, batch, batch, P(), in_weights, out_weights),
        out_specs=(batch, in_weights, out_weights),
        check_vma=False,
    )
```

```python
import jax
import jax.numpy as jnp
from jax import lax
from jax.experimental import pallas as pl
from jax.experimental.pallas import tpu as pltpu
from jax.sharding import Mesh, PartitionSpec as P

coeff = 0.7978845608028654
Y_LO, X, Z, Y_HI, CORE = 4, 4, 12, 2, 2
EXPERT_AXES = ("z", "yh", "c")
LANES = 128


def gelu_pair(pre):
    square = pre * pre
    tanh_val = jnp.tanh(pre * (coeff + (coeff * 0.044715) * square))
    share = 0.5 + 0.5 * tanh_val
    act = pre * share
    slope = share + (0.5 * pre) * (1.0 - tanh_val * tanh_val) * (
        coeff + (coeff * 3.0 * 0.044715) * square
    )
    return (act, slope)


def turn(value, axis, amount):
    size = lax.axis_size(axis)
    return lax.ppermute(value, axis, [(i, (i + amount) % size) for i in range(size)])


def rowdot(left, right):
    return lax.dot_general(
        left, right, (((0,), (0,)), ((), ())), preferred_element_type=jnp.float32
    )


def lanedot(left, right):
    return lax.dot_general(
        left, right, (((1,), (1,)), ((), ())), preferred_element_type=jnp.float32
    )


def expert_kernel(place, c0, c1, c2, win_in, wout_in, *refs):
    go_out, rows_out = refs[:2]
    dpre_out, part_out = refs[2], refs[3:7]
    rows, grads, win, wout, go, dpre, part, sems = refs[7:]
    slots = part.shape[0] // Y_LO
    step = win.shape[1] // X
    first = c0.shape[1]
    rest = slots - first
    used = []

    def copy(src, dst):
        used.append(pltpu.make_async_copy(src, dst, sems.at[len(used)]))
        used[-1].start()
        return used[-1]

    def near(axis, size, amount):
        return lax.rem(place[axis] + amount, size)

    row_loads, grad_loads, win_loads, wout_loads = [], [], [], []

    def load_weights(k):
        src = pl.ds(pl.multiple_of(near(1, X, k) * step, step), step)
        cols = pl.ds(k * step, step)
        win_loads.append(copy(win_in.at[near(1, X, k)], win.at[:, cols]))
        return lambda: wout_loads.append(copy(wout_in.at[src], wout.at[cols]))

    later = load_weights(0)
    for k in range(Y_LO):
        src = near(0, Y_LO, k)
        base = k * slots
        row_loads.append(copy(c0.at[src], rows.at[pl.ds(base, first)]))
        row_loads.append(copy(c1.at[src, pl.ds(0, rest)], rows.at[pl.ds(base + first, rest)]))
    after = [later] + [load_weights(k) for k in range(1, X)]
    for k in range(Y_LO):
        src = near(0, Y_LO, k)
        base = k * slots
        grad_loads.append(copy(c1.at[src, pl.ds(rest, rest)], grads.at[pl.ds(base, rest)]))
        grad_loads.append(copy(c2.at[src], grads.at[pl.ds(base + rest, first)]))
    for later in after:
        later()
    stores = []
    win_loads[0].wait()
    for load in row_loads:
        load.wait()
    pres = []
    for k in range(X):
        cols = pl.ds(k * step, step)
        if k:
            win_loads[k].wait()
        pres.append(jnp.dot(rows[...], win[:, cols], preferred_element_type=jnp.float32))
    for load in grad_loads + wout_loads:
        load.wait()
    dact = lanedot(grads[...], wout[...])
    for k in range(X):
        cols = pl.ds(k * step, step)
        act, slope = gelu_pair(pres[k])
        dpre[:, cols] = (dact[:, k * step : (k + 1) * step] * slope).astype(jnp.bfloat16)
        go[cols, :] = rowdot(act.astype(jnp.bfloat16), grads[...]).astype(jnp.bfloat16)
        dst = pl.ds(pl.multiple_of(near(1, X, k) * step, step), step)
        stores.append(copy(go.at[cols, :], go_out.at[dst]))
    stores.append(copy(rows, rows_out))
    stores.append(copy(dpre, dpre_out))
    part[...] = lanedot(dpre[...], win[...]).astype(jnp.bfloat16)
    for k in range(Y_LO):
        stores.append(copy(part.at[pl.ds(k * slots, slots)], part_out[k]))
    for store in stores:
        store.wait()


def expert_products(place, pieces, win, wout):
    _, first, width = pieces[0].shape
    hidden = wout.shape[0]
    slots = first * 3 // 2
    count = slots * Y_LO
    shapes = [(hidden, width), (count, width)]
    shapes += [(count, hidden)] + [(slots, width)] * Y_LO
    scratch = [(count, width)] * 2 + [(width, hidden), (hidden, width)]
    scratch += [(hidden, width), (count, hidden), (count, width)]
    anywhere = pl.BlockSpec(memory_space=pl.ANY)
    main = pl.BlockSpec(memory_space=pltpu.HBM)
    return pl.pallas_call(
        expert_kernel,
        out_shape=[jax.ShapeDtypeStruct(shape, jnp.bfloat16) for shape in shapes],
        in_specs=[pl.BlockSpec(memory_space=pltpu.SMEM)] + [anywhere] * 3 + [main] * 2,
        out_specs=[main] * (3 + Y_LO),
        scratch_shapes=[pltpu.VMEM(shape, jnp.bfloat16) for shape in scratch]
        + [pltpu.SemaphoreType.DMA((4 * Y_LO + 2 * X + 1 + X + 1 + Y_LO,))],
        compiler_params=pltpu.CompilerParams(vmem_limit_bytes=52 * 1024 * 1024),
        cost_estimate=pl.CostEstimate(
            flops=8 * count * width * hidden, bytes_accessed=11 << 20, transcendentals=count * hidden
        ),
    )(place, *pieces, win, wout)


def body(tokens, upstream, task_ids, task_expert, w_in, w_out):
    rows_dev, width = tokens.shape
    experts = task_expert.shape[0]
    capacity = max(2, (9 * rows_dev // 8 + experts - 1) // experts)
    slots = experts * capacity
    wide_in = lax.all_gather(w_in[0], "x", axis=0, tiled=False)
    wide_out = lax.all_gather(w_out[0], "x", axis=0, tiled=True)

    lanes = jnp.arange(experts, dtype=jnp.int32)
    task_hot = (task_ids == lanes[None, :]).astype(jnp.int32)
    target = jnp.sum(task_hot * task_expert[None, :], axis=1)
    dest_hot = (target[:, None] == lanes[None, :]).astype(jnp.int32)
    before = jnp.cumsum(dest_hot, axis=0) - dest_hot
    rank = jnp.sum(before * dest_hot, axis=1)
    slot = target * capacity + rank
    packer = (jnp.arange(slots, dtype=jnp.int32)[:, None] == slot[None, :]).astype(jnp.bfloat16)

    def pack(value):
        rows = jnp.dot(packer, value, preferred_element_type=jnp.float32).astype(jnp.bfloat16)
        return rows.reshape(experts, capacity * width // LANES, LANES)

    send = jnp.concatenate([pack(tokens), pack(upstream)], axis=1)
    got = lax.all_to_all(send, EXPERT_AXES, split_axis=0, concat_axis=0, tiled=True)
    half = capacity * width // LANES
    own = jnp.concatenate(
        [got[:, :half].reshape(slots, width), got[:, half:].reshape(slots, width)], axis=0
    )
    third = 2 * slots // 3
    pieces = [
        lax.all_gather(own[k * third : (k + 1) * third], "yl", axis=0, tiled=False)
        for k in range(3)
    ]
    place = jnp.stack([lax.axis_index("yl"), lax.axis_index("x")]).astype(jnp.int32)
    products = expert_products(place, pieces, wide_in, wide_out)
    part_out, rows = products[:2]
    dpre, pieces = products[2], products[3:]
    grad_out = lax.psum_scatter(part_out, "x", scatter_dimension=0, tiled=True)
    home = [turn(pieces[k], "yl", k) for k in (1, 2, 3)]

    block = w_in.shape[2]

    def own_block(k):
        return rowdot(rows, dpre[:, k * block : (k + 1) * block])

    def sent(k):
        return turn(own_block(k).astype(jnp.bfloat16), "x", k)

    one, three, two = sent(1), sent(3), sent(2)
    rows, one, three = lax.optimization_barrier((rows, one, three))
    near_sum = own_block(0) + one.astype(jnp.float32) + three.astype(jnp.float32)
    near_sum, two = lax.optimization_barrier((near_sum, two))
    grad_in = near_sum + two.astype(jnp.float32)

    total = pieces[0].astype(jnp.float32)
    for value in home:
        total = total + value.astype(jnp.float32)
    total = total.astype(jnp.bfloat16).reshape(experts, half, LANES)
    back = lax.all_to_all(total, EXPERT_AXES, split_axis=0, concat_axis=0, tiled=True)
    grad_out = grad_out.astype(jnp.float32)
    back, grad_out = lax.optimization_barrier((back, grad_out))
    token_grad = lax.dot_general(
        packer,
        back.reshape(slots, width),
        (((0,), (0,)), ((), ())),
        preferred_element_type=jnp.float32,
    ).astype(jnp.bfloat16)
    return (token_grad, grad_in[None], grad_out[None])


def solution(mesh):
    fine = Mesh(mesh.devices.reshape(Y_LO, X, Z, Y_HI, CORE), ("yl", "x") + EXPERT_AXES)
    batch = P(("yl", "x") + EXPERT_AXES, None)
    in_weights = P(EXPERT_AXES, None, ("yl", "x"))
    out_weights = P(EXPERT_AXES, ("yl", "x"), None)
    return jax.shard_map(
        body,
        mesh=fine,
        in_specs=(batch, batch, batch, P(), in_weights, out_weights),
        out_specs=(batch, in_weights, out_weights),
        check_vma=False,
    )
```

```python
import jax
import jax.numpy as jnp
from jax import lax
from jax.experimental import pallas as pl
from jax.experimental.pallas import tpu as pltpu
from jax.sharding import Mesh, PartitionSpec as P

coeff = 0.7978845608028654
Y_LO, X, Z, Y_HI, CORE = 4, 4, 12, 2, 2
EXPERT_AXES = ("z", "yh", "c")
LANES = 128


def gelu_pair(pre):
    square = pre * pre
    tanh_val = jnp.tanh(pre * (coeff + (coeff * 0.044715) * square))
    share = 0.5 + 0.5 * tanh_val
    act = pre * share
    slope = share + (0.5 * pre) * (1.0 - tanh_val * tanh_val) * (
        coeff + (coeff * 3.0 * 0.044715) * square
    )
    return (act, slope)


def turn(value, axis, amount):
    size = lax.axis_size(axis)
    return lax.ppermute(value, axis, [(i, (i + amount) % size) for i in range(size)])


def rowdot(left, right):
    return lax.dot_general(
        left, right, (((0,), (0,)), ((), ())), preferred_element_type=jnp.float32
    )


def lanedot(left, right):
    return lax.dot_general(
        left, right, (((1,), (1,)), ((), ())), preferred_element_type=jnp.float32
    )


def expert_kernel(place, c0, c1, c2, win_in, wout_in, *refs):
    go_out, rows_out = refs[:2]
    dpre_out, part_out = refs[2], refs[3:7]
    rows, grads, win, wout, go, dpre, part, sems = refs[7:]
    slots = part.shape[0] // Y_LO
    step = win.shape[1] // X
    first = c0.shape[1]
    rest = slots - first
    used = []

    def copy(src, dst):
        used.append(pltpu.make_async_copy(src, dst, sems.at[len(used)]))
        used[-1].start()
        return used[-1]

    def near(axis, size, amount):
        return lax.rem(place[axis] + amount, size)

    row_loads, grad_loads, win_loads, wout_loads = [], [], [], []

    def load_weights(k):
        src = pl.ds(pl.multiple_of(near(1, X, k) * step, step), step)
        cols = pl.ds(k * step, step)
        win_loads.append(copy(win_in.at[near(1, X, k)], win.at[:, cols]))
        return lambda: wout_loads.append(copy(wout_in.at[src], wout.at[cols]))

    later = load_weights(0)
    for k in range(Y_LO):
        src = near(0, Y_LO, k)
        base = k * slots
        row_loads.append(copy(c0.at[src], rows.at[pl.ds(base, first)]))
        row_loads.append(copy(c1.at[src, pl.ds(0, rest)], rows.at[pl.ds(base + first, rest)]))
    after = [later] + [load_weights(k) for k in range(1, X)]
    for k in range(Y_LO):
        src = near(0, Y_LO, k)
        base = k * slots
        grad_loads.append(copy(c1.at[src, pl.ds(rest, rest)], grads.at[pl.ds(base, rest)]))
        grad_loads.append(copy(c2.at[src], grads.at[pl.ds(base + rest, first)]))
    for later in after:
        later()
    stores = []
    win_loads[0].wait()
    for load in row_loads:
        load.wait()
    pres = []
    for k in range(X):
        cols = pl.ds(k * step, step)
        if k:
            win_loads[k].wait()
        pres.append(jnp.dot(rows[...], win[:, cols], preferred_element_type=jnp.float32))
    for load in grad_loads + wout_loads:
        load.wait()
    dact = lanedot(grads[...], wout[...])
    for k in range(X):
        cols = pl.ds(k * step, step)
        act, slope = gelu_pair(pres[k])
        dpre[:, cols] = (dact[:, k * step : (k + 1) * step] * slope).astype(jnp.bfloat16)
        go[cols, :] = rowdot(act.astype(jnp.bfloat16), grads[...]).astype(jnp.bfloat16)
        dst = pl.ds(pl.multiple_of(near(1, X, k) * step, step), step)
        stores.append(copy(go.at[cols, :], go_out.at[dst]))
    stores.append(copy(rows, rows_out))
    stores.append(copy(dpre, dpre_out))
    part[...] = lanedot(dpre[...], win[...]).astype(jnp.bfloat16)
    for k in range(Y_LO):
        stores.append(copy(part.at[pl.ds(k * slots, slots)], part_out[k]))
    for store in stores:
        store.wait()


def expert_products(place, pieces, win, wout):
    _, first, width = pieces[0].shape
    hidden = wout.shape[0]
    slots = first * 3 // 2
    count = slots * Y_LO
    shapes = [(hidden, width), (count, width)]
    shapes += [(count, hidden)] + [(slots, width)] * Y_LO
    scratch = [(count, width)] * 2 + [(width, hidden), (hidden, width)]
    scratch += [(hidden, width), (count, hidden), (count, width)]
    anywhere = pl.BlockSpec(memory_space=pl.ANY)
    main = pl.BlockSpec(memory_space=pltpu.HBM)
    return pl.pallas_call(
        expert_kernel,
        out_shape=[jax.ShapeDtypeStruct(shape, jnp.bfloat16) for shape in shapes],
        in_specs=[pl.BlockSpec(memory_space=pltpu.SMEM)] + [anywhere] * 3 + [main] * 2,
        out_specs=[main] * (3 + Y_LO),
        scratch_shapes=[pltpu.VMEM(shape, jnp.bfloat16) for shape in scratch]
        + [pltpu.SemaphoreType.DMA((4 * Y_LO + 2 * X + 1 + X + 1 + Y_LO,))],
        compiler_params=pltpu.CompilerParams(vmem_limit_bytes=52 * 1024 * 1024),
        cost_estimate=pl.CostEstimate(
            flops=8 * count * width * hidden, bytes_accessed=11 << 20, transcendentals=count * hidden
        ),
    )(place, *pieces, win, wout)


def body(tokens, upstream, task_ids, task_expert, w_in, w_out):
    rows_dev, width = tokens.shape
    experts = task_expert.shape[0]
    capacity = max(2, (9 * rows_dev // 8 + experts - 1) // experts)
    slots = experts * capacity
    wide_in = lax.all_gather(w_in[0], "x", axis=0, tiled=False)
    wide_out = lax.all_gather(w_out[0], "x", axis=0, tiled=True)

    lanes = jnp.arange(experts, dtype=jnp.int32)
    task_hot = (task_ids == lanes[None, :]).astype(jnp.int32)
    target = jnp.sum(task_hot * task_expert[None, :], axis=1)
    dest_hot = (target[:, None] == lanes[None, :]).astype(jnp.int32)
    before = jnp.cumsum(dest_hot, axis=0) - dest_hot
    rank = jnp.sum(before * dest_hot, axis=1)
    slot = target * capacity + rank
    packer = (jnp.arange(slots, dtype=jnp.int32)[:, None] == slot[None, :]).astype(jnp.bfloat16)

    def pack(value):
        rows = jnp.dot(packer, value, preferred_element_type=jnp.float32).astype(jnp.bfloat16)
        return rows.reshape(experts, capacity * width // LANES, LANES)

    send = jnp.concatenate([pack(tokens), pack(upstream)], axis=1)
    got = lax.all_to_all(send, EXPERT_AXES, split_axis=0, concat_axis=0, tiled=True)
    half = capacity * width // LANES
    own = jnp.concatenate(
        [got[:, :half].reshape(slots, width), got[:, half:].reshape(slots, width)], axis=0
    )
    third = 2 * slots // 3
    pieces = [
        lax.all_gather(own[k * third : (k + 1) * third], "yl", axis=0, tiled=False)
        for k in range(3)
    ]
    place = jnp.stack([lax.axis_index("yl"), lax.axis_index("x")]).astype(jnp.int32)
    products = expert_products(place, pieces, wide_in, wide_out)
    part_out, rows = products[:2]
    dpre, pieces = products[2], products[3:]
    grad_out = lax.psum_scatter(part_out, "x", scatter_dimension=0, tiled=True)
    home = [turn(pieces[k], "yl", k) for k in (1, 2, 3)]

    block = w_in.shape[2]

    def own_block(k):
        return rowdot(rows, dpre[:, k * block : (k + 1) * block])

    def sent(k):
        return turn(own_block(k).astype(jnp.bfloat16), "x", k)

    one, three, two = sent(1), sent(3), sent(2)
    rows, one, three = lax.optimization_barrier((rows, one, three))
    near_sum = own_block(0) + one.astype(jnp.float32) + three.astype(jnp.float32)
    grad_out = grad_out.astype(jnp.float32)
    near_sum, two, grad_out = lax.optimization_barrier((near_sum, two, grad_out))
    grad_in = near_sum + two.astype(jnp.float32)

    total = pieces[0].astype(jnp.float32)
    for value in home:
        total = total + value.astype(jnp.float32)
    total = total.astype(jnp.bfloat16).reshape(experts, half, LANES)
    back = lax.all_to_all(total, EXPERT_AXES, split_axis=0, concat_axis=0, tiled=True)
    back, grad_in = lax.optimization_barrier((back, grad_in))
    token_grad = lax.dot_general(
        packer,
        back.reshape(slots, width),
        (((0,), (0,)), ((), ())),
        preferred_element_type=jnp.float32,
    ).astype(jnp.bfloat16)
    return (token_grad, grad_in[None], grad_out[None])


def solution(mesh):
    fine = Mesh(mesh.devices.reshape(Y_LO, X, Z, Y_HI, CORE), ("yl", "x") + EXPERT_AXES)
    batch = P(("yl", "x") + EXPERT_AXES, None)
    in_weights = P(EXPERT_AXES, None, ("yl", "x"))
    out_weights = P(EXPERT_AXES, ("yl", "x"), None)
    return jax.shard_map(
        body,
        mesh=fine,
        in_specs=(batch, batch, batch, P(), in_weights, out_weights),
        out_specs=(batch, in_weights, out_weights),
        check_vma=False,
    )
```
